32 devices in a mesh: row: 4 (over x, core), col: 8 (over z, y).
Axes of the slice: x: 2, y: 2, z: 4, core: 2. Of those that a mesh axis runs over, the one named last changes fastest.
Arguments:
- density: bfloat16 [6144, 6144], P('row', 'col'), may hold values from -5 to 5
- strips: bfloat16 [1024, 8, 128], P(('row', 'col')), may hold values from -5 to 5
- dest_device: int32 [1024, 1], P(('row', 'col')), may hold values from 0 to 31; in each aligned block of 32 rows (0 to 31, 32 to 63, ...) at most 2 rows name the same one
- atom_slot: int32 [1024], P(('row', 'col')), may hold values from 0 to 191
- block_slot: int32 [1024], P(('row', 'col')), may hold values from 0 to 5
- patterns: int32 [3, 48, 48], replicated, may hold values 0 or 1
Outputs:
- density_next: float32 [6144, 6144], P('row', 'col')
- response_next: float32 [6144, 6144], P('row', 'col')
The draws below stay inside these ranges and needn't reach their ends.
Inputs may be any that keep to these rules, and one draw needn't show every extreme that they name: `dest_device`: of the 32 strips of one device, at most 2 name the same owner, and some owner is named that often.
All inputs are finite; a program needn't handle non-finite values.
Results may differ from the reference program's by a relative error of at most 0.0036.
Values may be sent and summed in bfloat16 or wider, within the bound.
No kernel may reach another device: no remote copies, remote signals or barrier semaphores. Data moves between devices by JAX's collectives and lax.ppermute only.
A program may use at most 128 MiB of HBM per device.

```python
import math
import jax
import jax.numpy as jnp
import numpy as np

ORB_BLOCK = 128
ATOM_ORB = 8
NB = 48
STEPS = 2
CAPACITY = 2
M = 6144
TR = 1536
TC = 768
ITEMS_DEV = 32
ITEMS = 1024
N_COL = 8
DEVICES = 32


def set_ends(result, own_key, smallest, high):
    longest = result.shape.index(max(result.shape))
    spots = []
    for shift in (0, 1):
        where = [jax.random.randint(jax.random.fold_in(own_key, axis), (), 0, length) for axis, length in enumerate(result.shape)]
        where[longest] = (where[longest] + shift) % result.shape[longest]
        spots.append(tuple(where))
    return result.at[spots[0]].set(smallest).at[spots[1]].set(high)


def steps_of(rng, dims, shards, least, largest):
    def one(position, parts):
        draws = jax.random.uniform(jax.random.fold_in(jax.random.fold_in(rng, 6), position), (parts,), jnp.float32, least / len(shards), largest / len(shards))
        return jnp.repeat(jnp.exp(draws), dims[position] // parts).reshape((-1,) + (1,) * (len(dims) - position - 1))

    factor_of = one(*shards[0])
    for cut in shards[1:]:
        factor_of = factor_of * one(*cut)
    return factor_of


def shared_out(stream_key, own, number, rows, amount, top, reach, slope):
    order = jax.random.permutation(stream_key, amount)
    heavy_load, ordinary = shares(amount, rows * top, reach, slope, True), shares(amount, rows * top, reach, slope, False)
    places = jnp.arange(amount)

    def named(tallies, rotation):
        used = int((tallies > 0).sum())
        fixed = max(1, used // 4)
        passed = fixed + (places - fixed + rotation * (used - fixed)) % max(1, amount - fixed)
        return jnp.zeros((amount,), jnp.int32).at[order[jnp.where(places < fixed, places, passed)]].set(jnp.asarray(tallies, jnp.int32))

    tallies = jnp.where(number % 4 == 0, named(heavy_load, number // 4), named(ordinary, number - number // 4 - 1))
    mixed = jax.random.permutation(jax.random.fold_in(own, 3), amount)
    source_of, sink = mixed[0:amount // 2 * 2:2], mixed[1:amount // 2 * 2:2]
    room = jnp.minimum(tallies[source_of] - 1, reach - tallies[sink]) // 2
    room = jnp.where((source_of == order[0]) | (sink == order[0]) | (tallies[sink] == 0), 0, jnp.maximum(room, 0))
    passed = jax.random.randint(jax.random.fold_in(own, 4), (amount // 2,), 0, 1 << 20) % (room + 1)
    tallies = tallies.at[source_of].add(-passed).at[sink].add(passed)
    labels = jnp.searchsorted(jnp.cumsum(tallies), jnp.arange(rows * top), side="right").astype(jnp.int32)
    listing = labels.reshape(top, rows).T
    listing = listing[jax.random.permutation(jax.random.fold_in(own, 1), rows)]
    rotation = jax.random.randint(jax.random.fold_in(own, 2), (rows, 1), 0, top)
    return jnp.take_along_axis(listing, (jnp.arange(top)[None, :] + rotation) % top, axis=1)


def shares(number_of, total, limit, lean, full):
    portions = [(1 << 20) // math.isqrt(rank ** lean) + 1 for rank in range(1, number_of + 1)]
    largest = limit if full else min(limit, max(-(-total // number_of), total * portions[0] // sum(portions)))
    least = 1 if total - largest >= number_of - 1 else 0
    given, spare = [largest] + [least] * (number_of - 1), total - largest - least * (number_of - 1)
    while spare > 0:
        candidates = [i for i in range(1, number_of) if given[i] < largest] or [i for i in range(1, number_of) if given[i] < limit]
        pool, budget = sum([portions[i] for i in candidates]), spare
        for i in candidates:
            addition = min(limit - given[i], max(1, budget * portions[i] // pool), spare)
            given[i] = given[i] + addition
            spare = spare - addition
    return np.array(given)


def scatter_about(own_key, extent, scale, most, pieces=(), kind=jnp.bfloat16):
    factor_of = steps_of(own_key, extent, pieces, -0.22, 0.18) if pieces else 1.0
    drawn = jax.random.normal(own_key, extent, jnp.float32) * scale * factor_of
    return jnp.minimum(jnp.maximum(drawn, -most), most).astype(kind)


def setup_inputs(seed: int = 0) -> dict:
    key_list = jax.random.split(jax.random.key(seed), 7)
    density = scatter_about(key_list[0], (M, M), 1.0, 5.0, ((0, 4), (1, 8)))
    strips = scatter_about(key_list[1], (ITEMS, ATOM_ORB, ORB_BLOCK), 1.0, 5.0, ((0, 32),))
    dest_device_keys = jax.random.split(jax.random.fold_in(key_list[2], 1), ITEMS // ITEMS_DEV)
    dest_device_turns = jax.random.permutation(jax.random.fold_in(key_list[2], 3), ITEMS // ITEMS_DEV)
    dest_device = jax.vmap(lambda own, number: shared_out(jax.random.fold_in(key_list[2], 2), own, number, ITEMS_DEV, DEVICES, 1, CAPACITY, 2))(dest_device_keys, dest_device_turns).reshape((ITEMS, 1))
    atom_slot = set_ends(jax.random.randint(key_list[3], (ITEMS,), 0, TR // ATOM_ORB), jax.random.fold_in(key_list[3], 1), 0, (TR // ATOM_ORB) - 1).astype(jnp.int32)
    block_slot = set_ends(jax.random.randint(key_list[4], (ITEMS,), 0, NB // N_COL), jax.random.fold_in(key_list[4], 1), 0, (NB // N_COL) - 1).astype(jnp.int32)
    patterns = set_ends((jax.random.randint(key_list[5], (3, NB, NB), 0, 5) < 3).astype(jnp.int32), jax.random.fold_in(key_list[5], 1), 0, 1)
    return dict(density=density, strips=strips, dest_device=dest_device, atom_slot=atom_slot, block_slot=block_slot, patterns=patterns)


def expand(pattern):
    diagonal = jnp.eye(NB, dtype=jnp.int32)
    kept = jnp.maximum(pattern, diagonal).astype(jnp.float32)
    return jnp.repeat(jnp.repeat(kept, ORB_BLOCK, axis=0), ORB_BLOCK, axis=1)

def reference(density, strips, dest_device, atom_slot, block_slot, patterns):
    kept_zero = expand(patterns[0])
    kept_first = expand(patterns[1])
    kept_field = expand(patterns[2])
    targets = dest_device[:, 0]
    atom_rows = targets // N_COL * (TR // ATOM_ORB) + atom_slot
    col_blocks = targets % N_COL * (TC // ORB_BLOCK) + block_slot
    field = jnp.zeros((M // ATOM_ORB, ATOM_ORB, NB, ORB_BLOCK), jnp.float32)
    field = field.at[atom_rows, :, col_blocks, :].add(strips.astype(jnp.float32))
    h_field = field.reshape(M, M)
    linear = (-(kept_field * h_field)).astype(jnp.bfloat16)
    zeroth = density
    inv_root = 1.0 / math.sqrt(M)
    new_zeroth = None
    new_linear = None
    for iteration in range(STEPS):
        square = jnp.dot(zeroth, zeroth, preferred_element_type=jnp.float32)
        crossed = jnp.dot(zeroth, linear, preferred_element_type=jnp.float32) + jnp.dot(linear, zeroth, preferred_element_type=jnp.float32)
        if iteration % 2 == 0:
            new_zeroth = kept_zero * (square * inv_root)
            new_linear = kept_first * (crossed * inv_root)
        else:
            new_zeroth = kept_zero * (2.0 * zeroth.astype(jnp.float32) - square * inv_root)
            new_linear = kept_first * (2.0 * linear.astype(jnp.float32) - crossed * inv_root)
        zeroth = new_zeroth.astype(jnp.bfloat16)
        linear = new_linear.astype(jnp.bfloat16)
    return (new_zeroth, new_linear)
```

```python
import functools
import math

import jax
import jax.numpy as jnp
from jax import lax
from jax.experimental import pallas as pl
from jax.experimental.pallas import tpu as pltpu
from jax.sharding import PartitionSpec as P

CAPACITY = 2
AXES = ("row", "col")
VMEM_BYTES = 56 * 1024 * 1024
COST_SHARE = 1


class Layout:
    def __init__(self, rows, cols):
        self.rows, self.cols = rows, cols
        self.nx, self.ny = rows // 2, cols // 4

    def index(self, x, k, zh, zl, y):
        return (2 * x + k) * self.cols + (2 * zh + zl) * self.ny + y

    def perm(self, source):
        pairs = []
        for x in range(self.nx):
            for k in range(2):
                for zh in range(2):
                    for zl in range(2):
                        for y in range(self.ny):
                            here = (x, k, zh, zl, y)
                            pairs.append((self.index(*source(*here)), self.index(*here)))
        return pairs

    def send(self, value, source):
        return lax.ppermute(value, AXES, self.perm(source))


def tie(*values):
    return lax.optimization_barrier(values)


class Rounds:
    def __init__(self, lay, **held):
        self.lay, self.held = lay, held

    def run(self, sends, **computed):
        held = dict(self.held, **computed)
        last = {}
        for link, name, source, route in sends:
            value = held[source]
            if link in last:
                value, held[last[link]] = tie(value, held[last[link]])
            held[name] = self.lay.send(value, route)
            last[link] = name
        self.held = dict(zip(held, tie(*held.values())))

    def __getitem__(self, name):
        return self.held[name]


def product(terms, mask, own, base, tile, scale, out_dtype, wait=(), span=None):
    height = sum(v.shape[0] for v in terms[0][0][0])
    width = terms[0][2][0][0].shape[1]
    order = sum(v.shape[0] for unit in terms[0][2] for v in unit)
    block = 128
    first_tile, end_tile = span or (0, height // tile)
    tiles = end_tile - first_tile
    arrays, plan_a, plan_b, places = [], [], [], []
    panels = 0
    for row_units, row_places, col_units, col_places in terms:
        if col_units is not None:
            for unit, place in zip(col_units, col_places):
                tall, first = sum(v.shape[0] for v in unit), 0
                for v in unit:
                    plan_b.append((panels, len(places), tall, first, len(arrays)))
                    arrays.append(v)
                    first += v.shape[0]
                places.append(place)
            panels += 1
        for unit, place in zip(row_units, row_places):
            first, parts = 0, []
            for v in unit:
                parts.append((len(arrays), first // tile, (first + v.shape[0]) // tile))
                arrays.append(v)
                first += v.shape[0]
            plan_a.append((panels - 1, len(places), unit[0].shape[1], parts))
            places.append(place)
    places = jnp.stack([jnp.asarray(p, jnp.int32) for p in places])
    count = len(arrays)
    deep = sum(wide for _, _, wide, _ in plan_a)

    def kernel(places_ref, *refs):
        refs = list(refs)
        del refs[: len(wait)]
        mask_ref = refs.pop(0) if mask is not None else None
        operands = [refs.pop(0) for _ in range(count)]
        own_ref = refs.pop(0) if own is not None else None
        base_ref = refs.pop(0) if base is not None else None
        out_ref, a_buf, b_buf, a_sem, b_sem = refs
        step = pl.program_id(0)
        slot = step % 2

        def row_copy(j, at, slot, act):
            offset = sum(wide for _, _, wide, _ in plan_a[:j])
            _, _, wide, parts = plan_a[j]
            for which, low, high in parts:
                if high <= first_tile or low >= end_tile:
                    continue

                def go():
                    start = pl.multiple_of((at - low) * tile, tile)
                    act(
                        pltpu.make_async_copy(
                            operands[which].at[pl.ds(start, tile), :],
                            a_buf.at[slot, :, pl.ds(offset, wide)],
                            a_sem.at[slot, j],
                        )
                    )

                if low <= first_tile and high >= end_tile:
                    go()
                else:
                    pl.when((at >= low) & (at < high))(go)

        def col_copy(j, act):
            panel, place, tall, first, which = plan_b[j]
            offset = pl.multiple_of(places_ref[place] * tall + first, 128)
            rows = pl.ds(offset, arrays[which].shape[0])
            act(pltpu.make_async_copy(operands[which], b_buf.at[panel, rows, :], b_sem.at[j]))

        @pl.when(step == 0)
        def _():
            for j in range(len(plan_b)):
                col_copy(j, lambda c: c.start())
            for j in range(len(plan_a)):
                row_copy(j, first_tile, 0, lambda c: c.start())

        @pl.when(step + 1 < tiles)
        def _():
            for j in range(len(plan_a)):
                row_copy(j, first_tile + step + 1, (step + 1) % 2, lambda c: c.start())

        @pl.when(step == 0)
        def _():
            for j in range(len(plan_b)):
                col_copy(j, lambda c: c.wait())

        for j in range(len(plan_a)):
            row_copy(j, first_tile + step, slot, lambda c: c.wait())
        total = None
        offset = 0
        for panel, place, wide, _ in plan_a:
            if wide == order:
                right = b_buf[panel]
            else:
                right = b_buf[panel, pl.ds(pl.multiple_of(places_ref[place] * wide, 128), wide), :]
            part = jnp.dot(a_buf[slot, :, offset : offset + wide], right, preferred_element_type=jnp.float32)
            total = part if total is None else total + part
            offset += wide
        if base is not None:
            total = total + base_ref[...]
        if mask is None:
            out_ref[...] = total
            return
        for i in range(tile // block):
            for j in range(width // block):
                at = (pl.ds(i * block, block), pl.ds(j * block, block))
                value = total[i * block : (i + 1) * block, j * block : (j + 1) * block] * scale
                if own is not None:
                    value = 2.0 * own_ref[at].astype(jnp.float32) - value
                kept = mask_ref[(first_tile + step) * (tile // block) + i, j]
                out_ref[at] = (value * kept).astype(out_dtype)

    smem = pl.BlockSpec(memory_space=pltpu.SMEM)
    tiled = pl.BlockSpec((tile, width), lambda i: (first_tile + i, 0))
    in_specs, operands = [smem], [places]
    in_specs, operands = in_specs + [pl.BlockSpec(memory_space=pl.ANY)] * len(wait), operands + list(wait)
    if mask is not None:
        in_specs, operands = in_specs + [smem], operands + [mask]
    in_specs = in_specs + [pl.BlockSpec(memory_space=pl.ANY)] * count
    operands = operands + arrays
    for extra in (own, base):
        if extra is not None:
            in_specs, operands = in_specs + [tiled], operands + [extra]
    return pl.pallas_call(
        kernel,
        grid=(tiles,),
        out_shape=jax.ShapeDtypeStruct((tiles * tile, width), out_dtype),
        in_specs=in_specs,
        out_specs=pl.BlockSpec((tile, width), lambda i: (i, 0)),
        scratch_shapes=[
            pltpu.VMEM((2, tile, deep), jnp.bfloat16),
            pltpu.VMEM((panels, order, width), jnp.bfloat16),
            pltpu.SemaphoreType.DMA((2, len(plan_a))),
            pltpu.SemaphoreType.DMA((len(plan_b),)),
        ],
        compiler_params=pltpu.CompilerParams(
            dimension_semantics=("arbitrary",), vmem_limit_bytes=VMEM_BYTES
        ),
        cost_estimate=pl.CostEstimate(
            flops=2 * tiles * tile * width * deep // COST_SHARE,
            bytes_accessed=(2 * deep * height + 2 * panels * order * width + 4 * height * width) // COST_SHARE,
            transcendentals=0,
        ),
    )(*operands)


def field_panel(strips, tables, pattern, slabs, first, stride, block_row, block_col, height, width, along_rows):
    block = strips.shape[1]
    atom_width = 8
    senders, slots = tables.shape[1], tables.shape[2]
    sent = strips.shape[0] // senders
    scalars = jnp.stack([jnp.asarray(v, jnp.int32) for v in (block_row, block_col, first)])
    tall, wide = height // block, width // block

    def kernel(scalar_ref, table_ref, pattern_ref, strips_ref, out_ref, field):
        step = pl.program_id(0)
        owner = (scalar_ref[2] + step * stride) * CAPACITY
        field[...] = jnp.zeros(field.shape, field.dtype)

        def one(sender, carry):
            for rank in range(CAPACITY):
                source = table_ref[0, sender, owner + rank]

                @pl.when(source >= 0)
                def _():
                    pair = lax.div(source, 2)
                    start = pl.multiple_of(sender * sent + pair * (2 * atom_width), 2 * atom_width)
                    both = strips_ref[pl.ds(start, 2 * atom_width), :].astype(jnp.float32)
                    strip = jnp.where(source > 2 * pair, both[atom_width:], both[:atom_width])
                    row = pl.multiple_of(table_ref[1, sender, owner + rank] * atom_width, atom_width)
                    col = pl.multiple_of(table_ref[2, sender, owner + rank] * block, block)
                    at = (pl.ds(row, atom_width), pl.ds(col, block))
                    field[at] = field[at] + strip

            return carry

        lax.fori_loop(0, senders, one, 0)
        first_row = scalar_ref[0] + (0 if along_rows else step * tall)
        first_col = scalar_ref[1] + (step * wide if along_rows else 0)
        for i in range(tall):
            for j in range(wide):
                at = (pl.ds(i * block, block), pl.ds(j * block, block))
                row, col = first_row + i, first_col + j
                kept = jnp.where((pattern_ref[row, col] > 0) | (row == col), -1.0, 0.0)
                out_ref[at] = (field[at] * kept).astype(out_ref.dtype)

    smem = pl.BlockSpec(memory_space=pltpu.SMEM)
    if along_rows:
        shape, out_spec = (height, slabs * width), pl.BlockSpec((height, width), lambda s: (0, s))
    else:
        shape, out_spec = (slabs * height, width), pl.BlockSpec((height, width), lambda s: (s, 0))
    return pl.pallas_call(
        kernel,
        grid=(slabs,),
        out_shape=jax.ShapeDtypeStruct(shape, jnp.bfloat16),
        in_specs=[smem, smem, smem, pl.BlockSpec(strips.shape, lambda s: (0, 0), pipeline_mode=pl.Buffered(1))],
        out_specs=out_spec,
        scratch_shapes=[pltpu.VMEM((height, width), jnp.float32)],
        compiler_params=pltpu.CompilerParams(
            dimension_semantics=("arbitrary",), vmem_limit_bytes=VMEM_BYTES
        ),
        cost_estimate=pl.CostEstimate(
            flops=slabs * height * width * 8, bytes_accessed=slabs * height * width * 8, transcendentals=0
        ),
    )(scalars, tables, pattern, strips)


def gather_strips(strips, targets, atoms, blocks, devices):
    count, atom_width, block = strips.shape
    matches = targets[:, None] == lax.iota(jnp.int32, devices)[None, :]
    before = jnp.cumsum(matches.astype(jnp.int32), axis=0) - 1
    lists = []
    for value in (lax.iota(jnp.int32, count), atoms, blocks):
        picked = [
            jnp.max(jnp.where(matches & (before == rank), value[:, None], -1), axis=0) for rank in range(CAPACITY)
        ]
        lists.append(jnp.stack(picked, axis=1).reshape(-1))
    table = jnp.stack(lists)
    slots = devices * CAPACITY
    lines = -(-3 * slots // block)
    lines = -(-lines // 16) * 16
    table = jnp.pad(table.reshape(-1), (0, lines * block - 3 * slots)).reshape(lines, block)
    sent = jnp.concatenate([strips.reshape(count * atom_width, block), table.astype(strips.dtype)])
    rows = sent.shape[0]
    all_sent = lax.all_gather(sent, AXES, axis=0, tiled=True)
    tables = all_sent.reshape(devices, rows, block)[:, count * atom_width :]
    tables = tables.astype(jnp.int32).reshape(devices, -1)[:, : 3 * slots]
    return all_sent, tables.reshape(devices, 3, slots).transpose(1, 0, 2)


def kept_blocks(pattern, first_row, first_col, tall, wide):
    window = lax.dynamic_slice(pattern, (first_row, first_col), (tall, wide))
    rows = first_row + lax.iota(jnp.int32, tall)
    cols = first_col + lax.iota(jnp.int32, wide)
    return jnp.maximum(window, (rows[:, None] == cols[None, :]).astype(jnp.int32)).astype(jnp.float32)


def on_device(density, strips, dest_device, atom_slot, block_slot, patterns):
    height, width = density.shape
    lay = Layout(lax.axis_size("row"), lax.axis_size("col"))
    nx, ny = lay.nx, lay.ny
    devices = lay.rows * lay.cols
    order = height * lay.rows
    block = strips.shape[2]
    tall, wide = height // block, width // block
    tile = 256
    inv_root = 1.0 / math.sqrt(order)

    row, col = lax.axis_index("row"), lax.axis_index("col")
    x, k = row // 2, row % 2
    zh, zl, y = col // (2 * ny), (col // ny) % 2, col % ny
    my_row = 2 * x + zl
    my_col = (2 * zh + k) * ny + y
    own_places = [(2 * zh + b) * ny + (y + s) % ny for b in (k, 1 - k) for s in range(ny)]
    far_places = [(2 * (1 - zh) + b) * ny + (y + s) % ny for b in (k, 1 - k) for s in range(ny)]
    row_places = own_places + far_places
    col_places = [2 * ((x + s) % nx) + b for b in (zl, 1 - zl) for s in range(nx)]
    kept_zero = kept_blocks(patterns[0], my_row * tall, my_col * wide, tall, wide)
    kept_first = kept_blocks(patterns[1], my_row * tall, my_col * wide, tall, wide)

    to_x = lambda x, k, zh, zl, y: ((x + 1) % nx, k, zh, zl, y)
    to_y = lambda x, k, zh, zl, y: (x, k, zh, zl, (y + 1) % ny)
    to_core = lambda x, k, zh, zl, y: (x, 1 - k, zh, zl, y)
    to_zh = lambda x, k, zh, zl, y: (x, k, 1 - zh, zl, y)
    to_zl = lambda x, k, zh, zl, y: (x, k, zh, 1 - zl, y)
    swap = lambda x, k, zh, zl, y: (x, zl, zh, k, y)

    def cut(v, *heights):
        ends = [0]
        for h in heights:
            ends.append(ends[-1] + h)
        return [v[p:q] for p, q in zip(ends, ends[1:])]

    def partial(rows, places, cols, col_places, base=None, wait=()):
        return product([(rows, places, cols, col_places)], None, None, base, tile, 1.0, jnp.float32, wait)

    def finish(terms, kept, own, base, wait=(), span=None):
        return product(terms, kept, own, base, tile, inv_root, jnp.bfloat16, wait, span)

    half = height // tile // 2 * tile
    most = height // tile * 2 // 3 * tile

    def along_x(unit):
        return [unit] + [f"{unit}_x{s}" for s in range(1, nx)]

    def along_y(unit):
        return [unit] + [f"{unit}_y{s}" for s in range(1, ny)]

    def sends_x(*units):
        return [("x", b, a, to_x) for u in units for a, b in zip(along_x(u), along_x(u)[1:])]

    def sends_y(*units):
        return [("y", b, a, to_y) for u in units for a, b in zip(along_y(u), along_y(u)[1:])]

    def sends_core(*units):
        return [("core", u + "_k", u, to_core) for u in units]

    def rest_core(*units):
        return sends_core(*[u for unit in units for u in along_y(unit)[1:]])

    def rows_of(*chunks):
        units = [list(unit) for unit in zip(*[along_y(u) for u in chunks])]
        units = units + [[u + "_k" for u in unit] for unit in units]
        return [[r[u] for u in unit] for unit in units]

    def cols_of(*chunks):
        return [[r[u] for u in unit] for unit in zip(*[along_x(u) for u in chunks])]

    r = Rounds(lay)
    v0, v1 = cut(density, half, height - half)
    r.held = dict(density=density, v0=v0, v1=v1)
    from_far = lambda x, k, zh, zl, y: (x, zl, 1 - zh, k, y)
    from_beside = lambda x, k, zh, zl, y: (x, 1 - zl, zh, k, y)
    r.run([("zh", "f0", "v0", from_far), ("zl", "own", "density", swap)])
    all_strips, tables = gather_strips(strips, dest_device[:, 0], atom_slot, block_slot, devices)
    r.run(
        [("zh", "f1", "v1", from_far), ("zl", "zl", "density", from_beside)]
        + sends_x("own")
        + sends_y("own")
        + sends_core("own")
    )
    r.run(sends_x("zl") + sends_y("f0", "f1") + rest_core("own") + sends_core("f0", "f1") + rest_core("f0"))
    zero_cols = cols_of("own") + cols_of("zl")
    base = partial(rows_of("own"), own_places, zero_cols, col_places)
    r.run(rest_core("f1"), base=base)
    zero_cols = cols_of("own") + cols_of("zl")
    far_rows = rows_of("f0", "f1")
    old_rows = rows_of("own") + far_rows
    zeroth = finish([(far_rows, far_places, zero_cols, col_places)], kept_zero, None, r["base"])

    tables, zeroth = tie(tables, zeroth)
    field_cols = field_panel(
        all_strips, tables, patterns[2], lay.rows, my_col, lay.cols, 0, my_col * wide, height, width, False
    )
    field_rows = field_panel(
        all_strips, tables, patterns[2], lay.cols, my_row * lay.cols, 1, my_row * tall, 0, height, width, True
    )

    def start(v, tag):
        one, two = cut(v, most, height - most)
        return {"own" + tag: v, "v0" + tag: one, "v1" + tag: two}

    def first_sends(tag):
        return (
            [("zh", "f0" + tag, "v0" + tag, to_zh), ("zl", "z0" + tag, "v0" + tag, to_zl)]
            + sends_x("own" + tag)
            + sends_y("own" + tag)
            + sends_core("own" + tag)
        )

    def second_sends(tag):
        return (
            [("zh", "f1" + tag, "v1" + tag, to_zh), ("zl", "z1" + tag, "v1" + tag, to_zl)]
            + sends_x("z0" + tag)
            + sends_y("f0" + tag)
            + rest_core("own" + tag)
            + sends_core("f0" + tag)
        )

    def third_sends(tag):
        return sends_x("z1" + tag) + sends_y("f1" + tag) + sends_core("f1" + tag) + rest_core("f0" + tag)

    def col_panel(tag):
        return cols_of("own" + tag) + cols_of("z0" + tag, "z1" + tag)

    r = Rounds(lay)
    r.held = start(zeroth, "p")
    first = partial(old_rows, row_places, [[field_cols]], [0], None, (zeroth,))
    linear = finish([([[field_rows]], [0], zero_cols, col_places)], kept_first, None, first)
    r.run(first_sends("p"), linear=linear)
    r.run(second_sends("p"))
    r.held.update(start(r["linear"], "q"))
    r.run(third_sends("p") + rest_core("f1p") + first_sends("q"))
    zero_rows = rows_of("ownp") + rows_of("f0p", "f1p")
    new_zeroth = finish([(zero_rows, row_places, col_panel("p"), col_places)], kept_zero, r["ownp"], None)
    r.run(second_sends("q"), new_zeroth=new_zeroth)
    base = partial(rows_of("ownq"), own_places, col_panel("p"), col_places)
    r.run([("zl", "back", "new_zeroth", swap)] + third_sends("q"), base=base)
    zero_rows = rows_of("ownp") + rows_of("f0p", "f1p")
    spans = ((0, most // tile), (most // tile, height // tile))

    def last(far_rows, base, span):
        terms = [
            (zero_rows, row_places, col_panel("q"), col_places),
            (far_rows, far_places, col_panel("p"), col_places),
        ]
        return finish(terms, kept_first, r["ownq"], base, (), span)

    far_rows = rows_of("f0q")
    top = last(far_rows, r["base"], spans[0])
    r.run(rest_core("f1q"), top=top)
    back_top = lay.send(r["top"], swap)
    bottom = last(rows_of("f0q", "f1q"), r["base"], spans[1])
    back_bottom = lay.send(bottom, swap)
    new_linear = jnp.concatenate([back_top, back_bottom]).astype(jnp.float32)
    return (r["back"].astype(jnp.float32), new_linear)


def solution(mesh):
    return jax.shard_map(
        on_device,
        mesh=mesh,
        in_specs=(
            P("row", "col"),
            P(("row", "col"), None, None),
            P(("row", "col"), None),
            P(("row", "col")),
            P(("row", "col")),
            P(),
        ),
        out_specs=(P("row", "col"), P("row", "col")),
        check_vma=False,
    )
```

```python
import functools
import math

import jax
import jax.numpy as jnp
from jax import lax
from jax.experimental import pallas as pl
from jax.experimental.pallas import tpu as pltpu
from jax.sharding import PartitionSpec as P

CAPACITY = 2
AXES = ("row", "col")
VMEM_BYTES = 56 * 1024 * 1024
COST_SHARE = 1


class Layout:
    def __init__(self, rows, cols):
        self.rows, self.cols = rows, cols
        self.nx, self.ny = rows // 2, cols // 4

    def index(self, x, k, zh, zl, y):
        return (2 * x + k) * self.cols + (2 * zh + zl) * self.ny + y

    def perm(self, source):
        pairs = []
        for x in range(self.nx):
            for k in range(2):
                for zh in range(2):
                    for zl in range(2):
                        for y in range(self.ny):
                            here = (x, k, zh, zl, y)
                            pairs.append((self.index(*source(*here)), self.index(*here)))
        return pairs

    def send(self, value, source):
        return lax.ppermute(value, AXES, self.perm(source))


def tie(*values):
    return lax.optimization_barrier(values)


class Rounds:
    def __init__(self, lay, **held):
        self.lay, self.held = lay, held

    def run(self, sends, **computed):
        held = dict(self.held, **computed)
        last = {}
        for link, name, source, route in sends:
            value = held[source]
            if link in last:
                value, held[last[link]] = tie(value, held[last[link]])
            held[name] = self.lay.send(value, route)
            last[link] = name
        self.held = dict(zip(held, tie(*held.values())))

    def __getitem__(self, name):
        return self.held[name]


def product(terms, mask, own, base, tile, scale, out_dtype, wait=(), span=None):
    height = sum(v.shape[0] for v in terms[0][0][0])
    width = terms[0][2][0][0].shape[1]
    order = sum(v.shape[0] for unit in terms[0][2] for v in unit)
    block = 128
    first_tile, end_tile = span or (0, height // tile)
    tiles = end_tile - first_tile
    arrays, plan_a, plan_b, places = [], [], [], []
    panels = 0
    for row_units, row_places, col_units, col_places in terms:
        places = places + [row_places, col_places]
        if col_units is not None:
            for place, unit in enumerate(col_units):
                place = (len(places) - 1, place)
                tall, first = sum(v.shape[0] for v in unit), 0
                for v in unit:
                    plan_b.append((panels, place, tall, first, len(arrays)))
                    arrays.append(v)
                    first += v.shape[0]
            panels += 1
        for place, unit in enumerate(row_units):
            first, parts = 0, []
            for v in unit:
                parts.append((len(arrays), first // tile, (first + v.shape[0]) // tile))
                arrays.append(v)
                first += v.shape[0]
            plan_a.append((panels - 1, (len(places) - 2, place), unit[0].shape[1], parts))
    count = len(arrays)
    deep = sum(wide for _, _, wide, _ in plan_a)

    def kernel(*refs):
        refs = list(refs)
        place_refs = [refs.pop(0) for _ in places]

        def place_of(which):
            return place_refs[which[0]][which[1]]

        del refs[: len(wait)]
        mask_ref = refs.pop(0) if mask is not None else None
        operands = [refs.pop(0) for _ in range(count)]
        own_ref = refs.pop(0) if own is not None else None
        base_ref = refs.pop(0) if base is not None else None
        out_ref, a_buf, b_buf, a_sem, b_sem = refs
        step = pl.program_id(0)
        slot = step % 2

        def row_copy(j, at, slot, act):
            offset = sum(wide for _, _, wide, _ in plan_a[:j])
            _, _, wide, parts = plan_a[j]
            for which, low, high in parts:
                if high <= first_tile or low >= end_tile:
                    continue

                def go():
                    start = pl.multiple_of((at - low) * tile, tile)
                    act(
                        pltpu.make_async_copy(
                            operands[which].at[pl.ds(start, tile), :],
                            a_buf.at[slot, :, pl.ds(offset, wide)],
                            a_sem.at[slot, j],
                        )
                    )

                if low <= first_tile and high >= end_tile:
                    go()
                else:
                    pl.when((at >= low) & (at < high))(go)

        def col_copy(j, act):
            panel, place, tall, first, which = plan_b[j]
            offset = pl.multiple_of(place_of(place) * tall + first, 128)
            rows = pl.ds(offset, arrays[which].shape[0])
            act(pltpu.make_async_copy(operands[which], b_buf.at[panel, rows, :], b_sem.at[j]))

        @pl.when(step == 0)
        def _():
            for j in range(len(plan_b)):
                col_copy(j, lambda c: c.start())
            for j in range(len(plan_a)):
                row_copy(j, first_tile, 0, lambda c: c.start())

        @pl.when(step + 1 < tiles)
        def _():
            for j in range(len(plan_a)):
                row_copy(j, first_tile + step + 1, (step + 1) % 2, lambda c: c.start())

        @pl.when(step == 0)
        def _():
            for j in range(len(plan_b)):
                col_copy(j, lambda c: c.wait())

        for j in range(len(plan_a)):
            row_copy(j, first_tile + step, slot, lambda c: c.wait())
        total = None
        offset = 0
        for panel, place, wide, _ in plan_a:
            if wide == order:
                right = b_buf[panel]
            else:
                right = b_buf[panel, pl.ds(pl.multiple_of(place_of(place) * wide, 128), wide), :]
            part = jnp.dot(a_buf[slot, :, offset : offset + wide], right, preferred_element_type=jnp.float32)
            total = part if total is None else total + part
            offset += wide
        if base is not None:
            total = total + base_ref[...]
        if mask is None:
            out_ref[...] = total
            return
        for i in range(tile // block):
            for j in range(width // block):
                at = (pl.ds(i * block, block), pl.ds(j * block, block))
                value = total[i * block : (i + 1) * block, j * block : (j + 1) * block] * scale
                if own is not None:
                    value = 2.0 * own_ref[at].astype(jnp.float32) - value
                kept = mask_ref[(first_tile + step) * (tile // block) + i, j]
                out_ref[at] = (value * kept).astype(out_dtype)

    smem = pl.BlockSpec(memory_space=pltpu.SMEM)
    tiled = pl.BlockSpec((tile, width), lambda i: (first_tile + i, 0))
    in_specs, operands = [smem] * len(places), list(places)
    in_specs, operands = in_specs + [pl.BlockSpec(memory_space=pl.ANY)] * len(wait), operands + list(wait)
    if mask is not None:
        in_specs, operands = in_specs + [smem], operands + [mask]
    in_specs = in_specs + [pl.BlockSpec(memory_space=pl.ANY)] * count
    operands = operands + arrays
    for extra in (own, base):
        if extra is not None:
            in_specs, operands = in_specs + [tiled], operands + [extra]
    return pl.pallas_call(
        kernel,
        grid=(tiles,),
        out_shape=jax.ShapeDtypeStruct((tiles * tile, width), out_dtype),
        in_specs=in_specs,
        out_specs=pl.BlockSpec((tile, width), lambda i: (i, 0)),
        scratch_shapes=[
            pltpu.VMEM((2, tile, deep), jnp.bfloat16),
            pltpu.VMEM((panels, order, width), jnp.bfloat16),
            pltpu.SemaphoreType.DMA((2, len(plan_a))),
            pltpu.SemaphoreType.DMA((len(plan_b),)),
        ],
        compiler_params=pltpu.CompilerParams(
            dimension_semantics=("arbitrary",), vmem_limit_bytes=VMEM_BYTES
        ),
        cost_estimate=pl.CostEstimate(
            flops=2 * tiles * tile * width * deep // COST_SHARE,
            bytes_accessed=(2 * deep * height + 2 * panels * order * width + 4 * height * width) // COST_SHARE,
            transcendentals=0,
        ),
    )(*operands)


def field_panel(strips, tables, pattern, slabs, first, stride, block_row, block_col, height, width, along_rows):
    block = strips.shape[1]
    atom_width = 8
    senders, slots = tables.shape[1], tables.shape[2]
    sent = strips.shape[0] // senders
    scalars = jnp.stack([jnp.asarray(v, jnp.int32) for v in (block_row, block_col, first)])
    tall, wide = height // block, width // block

    def kernel(scalar_ref, table_ref, pattern_ref, strips_ref, out_ref, field):
        step = pl.program_id(0)
        owner = (scalar_ref[2] + step * stride) * CAPACITY
        field[...] = jnp.zeros(field.shape, field.dtype)

        def one(sender, carry):
            for rank in range(CAPACITY):
                source = table_ref[0, sender, owner + rank]

                @pl.when(source >= 0)
                def _():
                    pair = lax.div(source, 2)
                    start = pl.multiple_of(sender * sent + pair * (2 * atom_width), 2 * atom_width)
                    both = strips_ref[pl.ds(start, 2 * atom_width), :].astype(jnp.float32)
                    strip = jnp.where(source > 2 * pair, both[atom_width:], both[:atom_width])
                    row = pl.multiple_of(table_ref[1, sender, owner + rank] * atom_width, atom_width)
                    col = pl.multiple_of(table_ref[2, sender, owner + rank] * block, block)
                    at = (pl.ds(row, atom_width), pl.ds(col, block))
                    field[at] = field[at] + strip

            return carry

        lax.fori_loop(0, senders, one, 0)
        first_row = scalar_ref[0] + (0 if along_rows else step * tall)
        first_col = scalar_ref[1] + (step * wide if along_rows else 0)
        for i in range(tall):
            for j in range(wide):
                at = (pl.ds(i * block, block), pl.ds(j * block, block))
                row, col = first_row + i, first_col + j
                kept = jnp.where((pattern_ref[row, col] > 0) | (row == col), -1.0, 0.0)
                out_ref[at] = (field[at] * kept).astype(out_ref.dtype)

    smem = pl.BlockSpec(memory_space=pltpu.SMEM)
    if along_rows:
        shape, out_spec = (height, slabs * width), pl.BlockSpec((height, width), lambda s: (0, s))
    else:
        shape, out_spec = (slabs * height, width), pl.BlockSpec((height, width), lambda s: (s, 0))
    return pl.pallas_call(
        kernel,
        grid=(slabs,),
        out_shape=jax.ShapeDtypeStruct(shape, jnp.bfloat16),
        in_specs=[smem, smem, smem, pl.BlockSpec(strips.shape, lambda s: (0, 0), pipeline_mode=pl.Buffered(1))],
        out_specs=out_spec,
        scratch_shapes=[pltpu.VMEM((height, width), jnp.float32)],
        compiler_params=pltpu.CompilerParams(
            dimension_semantics=("arbitrary",), vmem_limit_bytes=VMEM_BYTES
        ),
        cost_estimate=pl.CostEstimate(
            flops=slabs * height * width * 8, bytes_accessed=slabs * height * width * 8, transcendentals=0
        ),
    )(scalars, tables, pattern, strips)


def to_send(strips, targets, atoms, blocks, devices):
    count, atom_width, block = strips.shape
    matches = targets[:, None] == lax.iota(jnp.int32, devices)[None, :]
    before = jnp.cumsum(matches.astype(jnp.int32), axis=0) - 1
    lists = []
    for value in (lax.iota(jnp.int32, count), atoms, blocks):
        picked = [
            jnp.max(jnp.where(matches & (before == rank), value[:, None], -1), axis=0) for rank in range(CAPACITY)
        ]
        lists.append(jnp.stack(picked, axis=1).reshape(-1))
    table = jnp.stack(lists)
    slots = devices * CAPACITY
    lines = -(-3 * slots // block)
    lines = -(-lines // 16) * 16
    table = jnp.pad(table.reshape(-1), (0, lines * block - 3 * slots)).reshape(lines, block)
    return jnp.concatenate([strips.reshape(count * atom_width, block), table.astype(strips.dtype)])


def gather_strips(sent, lines, devices):
    slots, block = devices * CAPACITY, sent.shape[1]
    all_sent = lax.all_gather(sent, AXES, axis=0, tiled=True)
    tables = all_sent.reshape(devices, -1, block)[:, lines:]
    tables = tables.astype(jnp.int32).reshape(devices, -1)[:, : 3 * slots]
    return all_sent, tables.reshape(devices, 3, slots).transpose(1, 0, 2)


def kept_blocks(pattern, first_row, first_col, tall, wide):
    window = lax.dynamic_slice(pattern, (first_row, first_col), (tall, wide))
    rows = first_row + lax.iota(jnp.int32, tall)
    cols = first_col + lax.iota(jnp.int32, wide)
    return jnp.maximum(window, (rows[:, None] == cols[None, :]).astype(jnp.int32)).astype(jnp.float32)


def on_device(density, strips, dest_device, atom_slot, block_slot, patterns):
    height, width = density.shape
    lay = Layout(lax.axis_size("row"), lax.axis_size("col"))
    nx, ny = lay.nx, lay.ny
    devices = lay.rows * lay.cols
    order = height * lay.rows
    block = strips.shape[2]
    tall, wide = height // block, width // block
    tile = 256
    inv_root = 1.0 / math.sqrt(order)

    row, col = lax.axis_index("row"), lax.axis_index("col")
    x, k = row // 2, row % 2
    zh, zl, y = col // (2 * ny), (col // ny) % 2, col % ny
    my_row = 2 * x + zl
    my_col = (2 * zh + k) * ny + y
    own_places = [(2 * zh + b) * ny + (y + s) % ny for b in (k, 1 - k) for s in range(ny)]
    far_places = [(2 * (1 - zh) + b) * ny + (y + s) % ny for b in (k, 1 - k) for s in range(ny)]
    row_places = own_places + far_places
    col_places = [2 * ((x + s) % nx) + b for b in (zl, 1 - zl) for s in range(nx)]
    kept_zero = kept_blocks(patterns[0], my_row * tall, my_col * wide, tall, wide)
    kept_first = kept_blocks(patterns[1], my_row * tall, my_col * wide, tall, wide)

    to_x = lambda x, k, zh, zl, y: ((x + 1) % nx, k, zh, zl, y)
    to_y = lambda x, k, zh, zl, y: (x, k, zh, zl, (y + 1) % ny)
    to_core = lambda x, k, zh, zl, y: (x, 1 - k, zh, zl, y)
    to_zh = lambda x, k, zh, zl, y: (x, k, 1 - zh, zl, y)
    to_zl = lambda x, k, zh, zl, y: (x, k, zh, 1 - zl, y)
    swap = lambda x, k, zh, zl, y: (x, zl, zh, k, y)

    def cut(v, *heights):
        ends = [0]
        for h in heights:
            ends.append(ends[-1] + h)
        return [v[p:q] for p, q in zip(ends, ends[1:])]

    def partial(rows, places, cols, col_places, base=None, wait=()):
        return product([(rows, places, cols, col_places)], None, None, base, tile, 1.0, jnp.float32, wait)

    def finish(terms, kept, own, base, wait=(), span=None):
        return product(terms, kept, own, base, tile, inv_root, jnp.bfloat16, wait, span)

    half = height // tile // 2 * tile

    def along_x(unit):
        return [unit] + [f"{unit}_x{s}" for s in range(1, nx)]

    def along_y(unit):
        return [unit] + [f"{unit}_y{s}" for s in range(1, ny)]

    def sends_x(*units):
        return [("x", b, a, to_x) for u in units for a, b in zip(along_x(u), along_x(u)[1:])]

    def sends_y(*units):
        return [("y", b, a, to_y) for u in units for a, b in zip(along_y(u), along_y(u)[1:])]

    def sends_core(*units):
        return [("core", u + "_k", u, to_core) for u in units]

    def rest_core(*units):
        return sends_core(*[u for unit in units for u in along_y(unit)[1:]])

    def rows_of(*chunks):
        units = [list(unit) for unit in zip(*[along_y(u) for u in chunks])]
        units = units + [[u + "_k" for u in unit] for unit in units]
        return [[r[u] for u in unit] for unit in units]

    def cols_of(*chunks):
        return [[r[u] for u in unit] for unit in zip(*[along_x(u) for u in chunks])]

    r = Rounds(lay)
    v0, v1 = cut(density, half, height - half)
    r.held = dict(
        density=density,
        v0=v0,
        v1=v1,
        sent=to_send(strips, dest_device[:, 0], atom_slot, block_slot, devices),
        own_at=jnp.stack(own_places),
        far_at=jnp.stack(far_places),
        row_at=jnp.stack(row_places),
        col_at=jnp.stack(col_places),
        kept_zero=kept_zero,
        kept_first=kept_first,
    )
    from_far = lambda x, k, zh, zl, y: (x, zl, 1 - zh, k, y)
    from_beside = lambda x, k, zh, zl, y: (x, 1 - zl, zh, k, y)
    r.run([("zh", "f0", "v0", from_far), ("zl", "own", "density", swap)])
    own_places, far_places, row_places, col_places = (r["own_at"], r["far_at"], r["row_at"], r["col_at"])
    kept_zero, kept_first = r["kept_zero"], r["kept_first"]
    r.run(
        [("zh", "f1", "v1", from_far), ("zl", "zl", "density", from_beside)]
        + sends_x("own")
        + sends_y("own")
        + sends_core("own")
    )
    all_strips, tables = gather_strips(r["sent"], strips.shape[0] * strips.shape[1], devices)
    r.run(sends_x("zl") + sends_y("f0", "f1") + rest_core("own") + sends_core("f0"))
    zero_cols = cols_of("own") + cols_of("zl")
    base = partial(rows_of("own"), own_places, zero_cols, col_places)
    apart = sends_core("f1") + rest_core("f0", "f1")
    r.run([(f"core{i}",) + send[1:] for i, send in enumerate(apart)], base=base)
    zero_cols = cols_of("own") + cols_of("zl")
    far_rows = rows_of("f0", "f1")
    old_rows = rows_of("own") + far_rows
    zeroth = finish([(far_rows, far_places, zero_cols, col_places)], kept_zero, None, r["base"])

    lone = jnp.zeros((1,), jnp.int32)
    tables, zeroth = tie(tables, zeroth)
    field_cols = field_panel(
        all_strips, tables, patterns[2], lay.rows, my_col, lay.cols, 0, my_col * wide, height, width, False
    )
    field_rows = field_panel(
        all_strips, tables, patterns[2], lay.cols, my_row * lay.cols, 1, my_row * tall, 0, height, width, True
    )

    tiles = height // tile
    few, some = max(1, tiles // 6), max(1, tiles // 3)
    parts = {"p": [tiles - some, some], "q": [few, tiles - some - few, some]}

    def start(v, tag):
        pieces = cut(v, *[part * tile for part in parts[tag]])
        return dict({f"v{i}{tag}": piece for i, piece in enumerate(pieces)}, **{"own" + tag: v})

    def sends_z(tag, i):
        return [("zh", f"f{i}{tag}", f"v{i}{tag}", to_zh), ("zl", f"z{i}{tag}", f"v{i}{tag}", to_zl)]

    def chunks(kind, tag):
        return [f"{kind}{i}{tag}" for i in range(len(parts[tag]))]

    def col_panel(tag):
        return cols_of("own" + tag) + cols_of(*chunks("z", tag))

    r = Rounds(lay)
    r.held = start(zeroth, "p")
    first = partial(old_rows, row_places, [[field_cols]], lone, None, (zeroth,))
    r.run(
        sends_z("p", 0) + sends_x("ownp") + sends_y("ownp") + sends_core("ownp"),
        first=first,
        field_rows=field_rows,
    )
    linear = finish([([[r["field_rows"]]], lone, zero_cols, col_places)], kept_first, None, r["first"])
    r.run(
        sends_z("p", 1) + sends_x("z0p") + sends_y("f0p") + rest_core("ownp") + sends_core("f0p"),
        **start(linear, "q"),
    )
    r.run(sends_z("q", 0) + sends_x("z1p") + sends_y("f1p") + sends_core("f1p") + rest_core("f0p"))
    r.run(sends_z("q", 1) + sends_x("ownq") + sends_y("ownq") + rest_core("f1p") + sends_core("ownq"))
    zero_rows = rows_of("ownp") + rows_of(*chunks("f", "p"))
    new_zeroth = finish([(zero_rows, row_places, col_panel("p"), col_places)], kept_zero, r["ownp"], None)
    r.run(
        sends_z("q", 2)
        + sends_x("z0q", "z1q")
        + sends_y("f0q", "f1q")
        + rest_core("ownq")
        + sends_core("f0q", "f1q"),
        new_zeroth=new_zeroth,
    )
    base = partial(rows_of("ownq"), own_places, col_panel("p"), col_places)
    r.run(sends_x("z2q") + sends_y("f2q") + sends_core("f2q") + rest_core("f0q", "f1q"), base=base)
    zero_rows = rows_of("ownp") + rows_of(*chunks("f", "p"))

    def last(far_rows, base, span):
        terms = [
            (zero_rows, row_places, col_panel("q"), col_places),
            (far_rows, far_places, col_panel("p"), col_places),
        ]
        return finish(terms, kept_first, r["ownq"], base, (), span)

    top = last(rows_of("f0q", "f1q"), r["base"], (0, tiles - some))
    r.run([("zl", "back", "new_zeroth", swap)] + rest_core("f2q"), top=top)
    back_top = lay.send(r["top"], swap)
    bottom = last(rows_of(*chunks("f", "q")), r["base"], (tiles - some, tiles))
    back_bottom = lay.send(bottom, swap)
    new_linear = jnp.concatenate([back_top, back_bottom]).astype(jnp.float32)
    return (r["back"].astype(jnp.float32), new_linear)


def solution(mesh):
    return jax.shard_map(
        on_device,
        mesh=mesh,
        in_specs=(
            P("row", "col"),
            P(("row", "col"), None, None),
            P(("row", "col"), None),
            P(("row", "col")),
            P(("row", "col")),
            P(),
        ),
        out_specs=(P("row", "col"), P("row", "col")),
        check_vma=False,
    )
```

```python
import functools
import math

import jax
import jax.numpy as jnp
from jax import lax
from jax.experimental import pallas as pl
from jax.experimental.pallas import tpu as pltpu
from jax.sharding import PartitionSpec as P

CAPACITY = 2
AXES = ("row", "col")
VMEM_BYTES = 56 * 1024 * 1024
COST_SHARE = 1


class Layout:
    def __init__(self, rows, cols):
        self.rows, self.cols = rows, cols
        self.nx, self.ny = rows // 2, cols // 4

    def index(self, x, k, zh, zl, y):
        return (2 * x + k) * self.cols + (2 * zh + zl) * self.ny + y

    def perm(self, source):
        pairs = []
        for x in range(self.nx):
            for k in range(2):
                for zh in range(2):
                    for zl in range(2):
                        for y in range(self.ny):
                            here = (x, k, zh, zl, y)
                            pairs.append((self.index(*source(*here)), self.index(*here)))
        return pairs

    def send(self, value, source):
        return lax.ppermute(value, AXES, self.perm(source))


def tie(*values):
    return lax.optimization_barrier(values)


class Rounds:
    def __init__(self, lay, **held):
        self.lay, self.held = lay, held

    def run(self, sends, **computed):
        held = dict(self.held, **computed)
        last = {}
        for link, name, source, route in sends:
            value = held[source]
            if link in last:
                value, held[last[link]] = tie(value, held[last[link]])
            held[name] = self.lay.send(value, route)
            last[link] = name
        self.held = dict(zip(held, tie(*held.values())))

    def __getitem__(self, name):
        return self.held[name]


def product(terms, mask, own, base, tile, scale, out_dtype, wait=(), span=None, cuts=()):
    height = sum(v.shape[0] for v in terms[0][0][0])
    width = terms[0][2][0][0].shape[1]
    order = sum(v.shape[0] for unit in terms[0][2] for v in unit)
    block = 128
    first_tile, end_tile = span or (0, height // tile)
    tiles = end_tile - first_tile
    ends = [sum(cuts[:i]) for i in range(len(cuts) + 1)]
    runs = list(zip(ends, ends[1:]))
    arrays, plan_a, plan_b, places = [], [], [], []
    panels = 0
    for row_units, row_places, col_units, col_places in terms:
        places = places + [row_places, col_places]
        if col_units is not None:
            for place, unit in enumerate(col_units):
                place = (len(places) - 1, place)
                tall, first = sum(v.shape[0] for v in unit), 0
                for v in unit:
                    plan_b.append((panels, place, tall, first, len(arrays)))
                    arrays.append(v)
                    first += v.shape[0]
            panels += 1
        for place, unit in enumerate(row_units):
            first, parts = 0, []
            for v in unit:
                parts.append((len(arrays), first // tile, (first + v.shape[0]) // tile))
                arrays.append(v)
                first += v.shape[0]
            plan_a.append((panels - 1, (len(places) - 2, place), unit[0].shape[1], parts))
    count = len(arrays)
    deep = sum(wide for _, _, wide, _ in plan_a)

    def kernel(*refs):
        refs = list(refs)
        place_refs = [refs.pop(0) for _ in places]

        def place_of(which):
            return place_refs[which[0]][which[1]]

        del refs[: len(wait)]
        mask_ref = refs.pop(0) if mask is not None else None
        operands = [refs.pop(0) for _ in range(count)]
        own_ref = refs.pop(0) if own is not None else None
        base_ref = refs.pop(0) if base is not None else None
        out_ref, *cut_refs, a_buf, b_buf, a_sem, b_sem = refs
        step = pl.program_id(0)
        slot = step % 2

        def row_copy(j, at, slot, act):
            offset = sum(wide for _, _, wide, _ in plan_a[:j])
            _, _, wide, parts = plan_a[j]
            for which, low, high in parts:
                if high <= first_tile or low >= end_tile:
                    continue

                def go():
                    start = pl.multiple_of((at - low) * tile, tile)
                    act(
                        pltpu.make_async_copy(
                            operands[which].at[pl.ds(start, tile), :],
                            a_buf.at[slot, :, pl.ds(offset, wide)],
                            a_sem.at[slot, j],
                        )
                    )

                if low <= first_tile and high >= end_tile:
                    go()
                else:
                    pl.when((at >= low) & (at < high))(go)

        def col_copy(j, act):
            panel, place, tall, first, which = plan_b[j]
            offset = pl.multiple_of(place_of(place) * tall + first, 128)
            rows = pl.ds(offset, arrays[which].shape[0])
            act(pltpu.make_async_copy(operands[which], b_buf.at[panel, rows, :], b_sem.at[j]))

        @pl.when(step == 0)
        def _():
            for j in range(len(plan_b)):
                col_copy(j, lambda c: c.start())
            for j in range(len(plan_a)):
                row_copy(j, first_tile, 0, lambda c: c.start())

        @pl.when(step + 1 < tiles)
        def _():
            for j in range(len(plan_a)):
                row_copy(j, first_tile + step + 1, (step + 1) % 2, lambda c: c.start())

        @pl.when(step == 0)
        def _():
            for j in range(len(plan_b)):
                col_copy(j, lambda c: c.wait())

        for j in range(len(plan_a)):
            row_copy(j, first_tile + step, slot, lambda c: c.wait())
        total = None
        offset = 0
        for panel, place, wide, _ in plan_a:
            if wide == order:
                right = b_buf[panel]
            else:
                right = b_buf[panel, pl.ds(pl.multiple_of(place_of(place) * wide, 128), wide), :]
            part = jnp.dot(a_buf[slot, :, offset : offset + wide], right, preferred_element_type=jnp.float32)
            total = part if total is None else total + part
            offset += wide
        if base is not None:
            total = total + base_ref[...]
        if mask is None:
            out_ref[...] = total
            return
        for i in range(tile // block):
            for j in range(width // block):
                at = (pl.ds(i * block, block), pl.ds(j * block, block))
                value = total[i * block : (i + 1) * block, j * block : (j + 1) * block] * scale
                if own is not None:
                    value = 2.0 * own_ref[at].astype(jnp.float32) - value
                kept = mask_ref[(first_tile + step) * (tile // block) + i, j]
                out_ref[at] = (value * kept).astype(out_dtype)
        for (low, high), cut_ref in zip(runs, cut_refs):

            @pl.when((step >= low) & (step < high))
            def _():
                cut_ref[...] = out_ref[...]

    smem = pl.BlockSpec(memory_space=pltpu.SMEM)
    out_shape = [jax.ShapeDtypeStruct((tiles * tile, width), out_dtype)]
    out_specs = [pl.BlockSpec((tile, width), lambda i: (i, 0))]
    for low, high in runs:
        out_shape.append(jax.ShapeDtypeStruct(((high - low) * tile, width), out_dtype))
        place = functools.partial(lambda low, high, i: (jnp.clip(i, low, high - 1) - low, 0), low, high)
        out_specs.append(pl.BlockSpec((tile, width), place))
    tiled = pl.BlockSpec((tile, width), lambda i: (first_tile + i, 0))
    in_specs, operands = [smem] * len(places), list(places)
    in_specs, operands = in_specs + [pl.BlockSpec(memory_space=pl.ANY)] * len(wait), operands + list(wait)
    if mask is not None:
        in_specs, operands = in_specs + [smem], operands + [mask]
    in_specs = in_specs + [pl.BlockSpec(memory_space=pl.ANY)] * count
    operands = operands + arrays
    for extra in (own, base):
        if extra is not None:
            in_specs, operands = in_specs + [tiled], operands + [extra]
    return pl.pallas_call(
        kernel,
        grid=(tiles,),
        out_shape=out_shape if cuts else out_shape[0],
        in_specs=in_specs,
        out_specs=out_specs if cuts else out_specs[0],
        scratch_shapes=[
            pltpu.VMEM((2, tile, deep), jnp.bfloat16),
            pltpu.VMEM((panels, order, width), jnp.bfloat16),
            pltpu.SemaphoreType.DMA((2, len(plan_a))),
            pltpu.SemaphoreType.DMA((len(plan_b),)),
        ],
        compiler_params=pltpu.CompilerParams(
            dimension_semantics=("arbitrary",), vmem_limit_bytes=VMEM_BYTES
        ),
        cost_estimate=pl.CostEstimate(
            flops=2 * tiles * tile * width * deep // COST_SHARE,
            bytes_accessed=(2 * deep * height + 2 * panels * order * width + 4 * height * width) // COST_SHARE,
            transcendentals=0,
        ),
    )(*operands)


def field_panel(strips, tables, pattern, slabs, first, stride, block_row, block_col, height, width, along_rows):
    block = strips.shape[1]
    atom_width = 8
    senders, slots = tables.shape[1], tables.shape[2]
    sent = strips.shape[0] // senders
    scalars = jnp.stack([jnp.asarray(v, jnp.int32) for v in (block_row, block_col, first)])
    tall, wide = height // block, width // block

    def kernel(scalar_ref, table_ref, pattern_ref, strips_ref, out_ref, field):
        step = pl.program_id(0)
        owner = (scalar_ref[2] + step * stride) * CAPACITY
        field[...] = jnp.zeros(field.shape, field.dtype)

        def one(sender, carry):
            for rank in range(CAPACITY):
                source = table_ref[0, sender, owner + rank]

                @pl.when(source >= 0)
                def _():
                    pair = lax.div(source, 2)
                    start = pl.multiple_of(sender * sent + pair * (2 * atom_width), 2 * atom_width)
                    both = strips_ref[pl.ds(start, 2 * atom_width), :].astype(jnp.float32)
                    strip = jnp.where(source > 2 * pair, both[atom_width:], both[:atom_width])
                    row = pl.multiple_of(table_ref[1, sender, owner + rank] * atom_width, atom_width)
                    col = pl.multiple_of(table_ref[2, sender, owner + rank] * block, block)
                    at = (pl.ds(row, atom_width), pl.ds(col, block))
                    field[at] = field[at] + strip

            return carry

        lax.fori_loop(0, senders, one, 0)
        first_row = scalar_ref[0] + (0 if along_rows else step * tall)
        first_col = scalar_ref[1] + (step * wide if along_rows else 0)
        for i in range(tall):
            for j in range(wide):
                at = (pl.ds(i * block, block), pl.ds(j * block, block))
                row, col = first_row + i, first_col + j
                kept = jnp.where((pattern_ref[row, col] > 0) | (row == col), -1.0, 0.0)
                out_ref[at] = (field[at] * kept).astype(out_ref.dtype)

    smem = pl.BlockSpec(memory_space=pltpu.SMEM)
    if along_rows:
        shape, out_spec = (height, slabs * width), pl.BlockSpec((height, width), lambda s: (0, s))
    else:
        shape, out_spec = (slabs * height, width), pl.BlockSpec((height, width), lambda s: (s, 0))
    return pl.pallas_call(
        kernel,
        grid=(slabs,),
        out_shape=jax.ShapeDtypeStruct(shape, jnp.bfloat16),
        in_specs=[smem, smem, smem, pl.BlockSpec(strips.shape, lambda s: (0, 0), pipeline_mode=pl.Buffered(1))],
        out_specs=out_spec,
        scratch_shapes=[pltpu.VMEM((height, width), jnp.float32)],
        compiler_params=pltpu.CompilerParams(
            dimension_semantics=("arbitrary",), vmem_limit_bytes=VMEM_BYTES
        ),
        cost_estimate=pl.CostEstimate(
            flops=slabs * height * width * 8, bytes_accessed=slabs * height * width * 8, transcendentals=0
        ),
    )(scalars, tables, pattern, strips)


def to_send(strips, targets, atoms, blocks, devices):
    count, atom_width, block = strips.shape
    matches = targets[:, None] == lax.iota(jnp.int32, devices)[None, :]
    before = jnp.cumsum(matches.astype(jnp.int32), axis=0) - 1
    lists = []
    for value in (lax.iota(jnp.int32, count), atoms, blocks):
        picked = [
            jnp.max(jnp.where(matches & (before == rank), value[:, None], -1), axis=0) for rank in range(CAPACITY)
        ]
        lists.append(jnp.stack(picked, axis=1).reshape(-1))
    table = jnp.stack(lists)
    slots = devices * CAPACITY
    lines = -(-3 * slots // block)
    lines = -(-lines // 16) * 16
    table = jnp.pad(table.reshape(-1), (0, lines * block - 3 * slots)).reshape(lines, block)
    return jnp.concatenate([strips.reshape(count * atom_width, block), table.astype(strips.dtype)])


def gather_strips(sent, lines, devices):
    slots, block = devices * CAPACITY, sent.shape[1]
    all_sent = lax.all_gather(sent, AXES, axis=0, tiled=True)
    tables = all_sent.reshape(devices, -1, block)[:, lines:]
    tables = tables.astype(jnp.int32).reshape(devices, -1)[:, : 3 * slots]
    return all_sent, tables.reshape(devices, 3, slots).transpose(1, 0, 2)


def kept_blocks(pattern, first_row, first_col, tall, wide):
    window = lax.dynamic_slice(pattern, (first_row, first_col), (tall, wide))
    rows = first_row + lax.iota(jnp.int32, tall)
    cols = first_col + lax.iota(jnp.int32, wide)
    return jnp.maximum(window, (rows[:, None] == cols[None, :]).astype(jnp.int32)).astype(jnp.float32)


def on_device(density, strips, dest_device, atom_slot, block_slot, patterns):
    height, width = density.shape
    lay = Layout(lax.axis_size("row"), lax.axis_size("col"))
    nx, ny = lay.nx, lay.ny
    devices = lay.rows * lay.cols
    order = height * lay.rows
    block = strips.shape[2]
    tall, wide = height // block, width // block
    tile = 256
    inv_root = 1.0 / math.sqrt(order)

    row, col = lax.axis_index("row"), lax.axis_index("col")
    x, k = row // 2, row % 2
    zh, zl, y = col // (2 * ny), (col // ny) % 2, col % ny
    my_row = 2 * x + zl
    my_col = (2 * zh + k) * ny + y
    own_places = [(2 * zh + b) * ny + (y + s) % ny for b in (k, 1 - k) for s in range(ny)]
    far_places = [(2 * (1 - zh) + b) * ny + (y + s) % ny for b in (k, 1 - k) for s in range(ny)]
    row_places = own_places + far_places
    col_places = [2 * ((x + s) % nx) + b for b in (zl, 1 - zl) for s in range(nx)]
    kept_zero = kept_blocks(patterns[0], my_row * tall, my_col * wide, tall, wide)
    kept_first = kept_blocks(patterns[1], my_row * tall, my_col * wide, tall, wide)

    to_x = lambda x, k, zh, zl, y: ((x + 1) % nx, k, zh, zl, y)
    to_y = lambda x, k, zh, zl, y: (x, k, zh, zl, (y + 1) % ny)
    to_core = lambda x, k, zh, zl, y: (x, 1 - k, zh, zl, y)
    to_zh = lambda x, k, zh, zl, y: (x, k, 1 - zh, zl, y)
    to_zl = lambda x, k, zh, zl, y: (x, k, zh, 1 - zl, y)
    swap = lambda x, k, zh, zl, y: (x, zl, zh, k, y)

    def cut(v, *heights):
        ends = [0]
        for h in heights:
            ends.append(ends[-1] + h)
        return [v[p:q] for p, q in zip(ends, ends[1:])]

    def partial(rows, places, cols, col_places, base=None, wait=()):
        return product([(rows, places, cols, col_places)], None, None, base, tile, 1.0, jnp.float32, wait)

    def finish(terms, kept, own, base, wait=(), span=None, cuts=()):
        return product(terms, kept, own, base, tile, inv_root, jnp.bfloat16, wait, span, cuts)

    half = height // tile // 2 * tile

    def along_x(unit):
        return [unit] + [f"{unit}_x{s}" for s in range(1, nx)]

    def along_y(unit):
        return [unit] + [f"{unit}_y{s}" for s in range(1, ny)]

    def sends_x(*units):
        return [("x", b, a, to_x) for u in units for a, b in zip(along_x(u), along_x(u)[1:])]

    def sends_y(*units):
        return [("y", b, a, to_y) for u in units for a, b in zip(along_y(u), along_y(u)[1:])]

    def sends_core(*units):
        return [("core", u + "_k", u, to_core) for u in units]

    def rest_core(*units):
        return sends_core(*[u for unit in units for u in along_y(unit)[1:]])

    def rows_of(*chunks):
        units = [list(unit) for unit in zip(*[along_y(u) for u in chunks])]
        units = units + [[u + "_k" for u in unit] for unit in units]
        return [[r[u] for u in unit] for unit in units]

    def cols_of(*chunks):
        return [[r[u] for u in unit] for unit in zip(*[along_x(u) for u in chunks])]

    r = Rounds(lay)
    v0, v1 = cut(density, half, height - half)
    r.held = dict(
        density=density,
        v0=v0,
        v1=v1,
        sent=to_send(strips, dest_device[:, 0], atom_slot, block_slot, devices),
        own_at=jnp.stack(own_places),
        far_at=jnp.stack(far_places),
        row_at=jnp.stack(row_places),
        col_at=jnp.stack(col_places),
        kept_zero=kept_zero,
        kept_first=kept_first,
    )
    from_far = lambda x, k, zh, zl, y: (x, zl, 1 - zh, k, y)
    from_beside = lambda x, k, zh, zl, y: (x, 1 - zl, zh, k, y)
    r.run([("zh", "f0", "v0", from_far), ("zl", "own", "density", swap)])
    own_places, far_places, row_places, col_places = (r["own_at"], r["far_at"], r["row_at"], r["col_at"])
    kept_zero, kept_first = r["kept_zero"], r["kept_first"]
    r.run(
        [("zh", "f1", "v1", from_far), ("zl", "zl", "density", from_beside)]
        + sends_x("own")
        + sends_y("own")
        + sends_core("own")
    )
    all_strips, tables = gather_strips(r["sent"], strips.shape[0] * strips.shape[1], devices)
    beside = [("y also",) + send[1:] for send in sends_y("f1")]
    r.run(sends_x("zl") + sends_y("f0") + beside + rest_core("own") + sends_core("f0"))
    zero_cols = cols_of("own") + cols_of("zl")
    base = partial(rows_of("own"), own_places, zero_cols, col_places)
    apart = sends_core("f1") + rest_core("f0", "f1")
    r.run([(f"core{i}",) + send[1:] for i, send in enumerate(apart)], base=base)
    zero_cols = cols_of("own") + cols_of("zl")
    far_rows = rows_of("f0", "f1")
    old_rows = rows_of("own") + far_rows
    tiles = height // tile
    few, some = max(1, tiles // 6), max(1, tiles // 3)
    parts = {"p": [tiles - some, some], "q": [few, tiles - some - few, some]}
    zeroth, v0, v1 = finish(
        [(far_rows, far_places, zero_cols, col_places)], kept_zero, None, r["base"], cuts=parts["p"]
    )

    lone = jnp.zeros((1,), jnp.int32)
    tables, zeroth = tie(tables, zeroth)
    field_cols = field_panel(
        all_strips, tables, patterns[2], lay.rows, my_col, lay.cols, 0, my_col * wide, height, width, False
    )
    field_rows = field_panel(
        all_strips, tables, patterns[2], lay.cols, my_row * lay.cols, 1, my_row * tall, 0, height, width, True
    )

    def start(v, tag):
        pieces = cut(v, *[part * tile for part in parts[tag]])
        return dict({f"v{i}{tag}": piece for i, piece in enumerate(pieces)}, **{"own" + tag: v})

    def sends_z(tag, i):
        return [("zh", f"f{i}{tag}", f"v{i}{tag}", to_zh), ("zl", f"z{i}{tag}", f"v{i}{tag}", to_zl)]

    def chunks(kind, tag):
        return [f"{kind}{i}{tag}" for i in range(len(parts[tag]))]

    def col_panel(tag):
        return cols_of("own" + tag) + cols_of(*chunks("z", tag))

    r = Rounds(lay)
    r.held = dict(ownp=zeroth, v0p=v0, v1p=v1)
    first = partial(old_rows, row_places, [[field_cols]], lone, None, (zeroth,))
    r.run(
        sends_z("p", 0) + sends_x("ownp") + sends_y("ownp") + sends_core("ownp"),
        first=first,
        field_rows=field_rows,
    )
    linear = finish([([[r["field_rows"]]], lone, zero_cols, col_places)], kept_first, None, r["first"])
    r.run(
        sends_z("p", 1) + sends_x("z0p") + sends_y("f0p") + rest_core("ownp") + sends_core("f0p"),
        **start(linear, "q"),
    )
    r.run(sends_z("q", 0) + sends_x("z1p") + sends_y("f1p") + sends_core("f1p") + rest_core("f0p"))
    r.run(sends_z("q", 1) + sends_x("ownq") + sends_y("ownq") + rest_core("f1p") + sends_core("ownq"))
    zero_rows = rows_of("ownp") + rows_of(*chunks("f", "p"))
    new_zeroth = finish([(zero_rows, row_places, col_panel("p"), col_places)], kept_zero, r["ownp"], None)
    r.run(
        sends_z("q", 2)
        + sends_x("z0q", "z1q")
        + sends_y("f0q", "f1q")
        + rest_core("ownq")
        + sends_core("f0q", "f1q"),
        new_zeroth=new_zeroth,
    )
    base = partial(rows_of("ownq"), own_places, col_panel("p"), col_places)
    r.run(sends_x("z2q") + sends_y("f2q") + sends_core("f2q") + rest_core("f0q", "f1q"), base=base)
    zero_rows = rows_of("ownp") + rows_of(*chunks("f", "p"))

    def last(far_rows, base, span):
        terms = [
            (zero_rows, row_places, col_panel("q"), col_places),
            (far_rows, far_places, col_panel("p"), col_places),
        ]
        return finish(terms, kept_first, r["ownq"], base, (), span)

    top = last(rows_of("f0q", "f1q"), r["base"], (0, tiles - some))
    r.run([("zl", "back", "new_zeroth", swap)] + rest_core("f2q"), top=top)
    back_top = lay.send(r["top"], swap)
    bottom = last(rows_of(*chunks("f", "q")), r["base"], (tiles - some, tiles))
    back_bottom = lay.send(bottom, swap)
    new_linear = jnp.concatenate([back_top, back_bottom]).astype(jnp.float32)
    return (r["back"].astype(jnp.float32), new_linear)


def solution(mesh):
    return jax.shard_map(
        on_device,
        mesh=mesh,
        in_specs=(
            P("row", "col"),
            P(("row", "col"), None, None),
            P(("row", "col"), None),
            P(("row", "col")),
            P(("row", "col")),
            P(),
        ),
        out_specs=(P("row", "col"), P("row", "col")),
        check_vma=False,
    )
```
